256 devices in a mesh: grp: 2 (over core), ep: 128 (over z, y, x).
Axes of the slice: x: 4, y: 4, z: 8, core: 2. Of those that a mesh axis runs over, the one named last changes fastest.
Arguments:
- activations: bfloat16 [32768, 2048], P(('grp', 'ep')), may hold values from -6 to 6
- out_grad: bfloat16 [32768, 2048], P(('grp', 'ep')), may hold values from -6 to 6
- expert_ids: int32 [32768, 4], P(('grp', 'ep')), may hold values from 0 to 127, all different within a row; in each aligned block of 128 rows (0 to 127, 128 to 255, ...) at most 5 rows name the same one
- gate_values: bfloat16 [32768, 4], P(('grp', 'ep')), may hold values from 0.049804688 to 1
- w_gate: bfloat16 [128, 2048, 768], P('ep', None, 'grp'), may hold values from -0.125 to 0.125
- w_up: bfloat16 [128, 2048, 768], P('ep', None, 'grp'), may hold values from -0.125 to 0.125
- w_down: bfloat16 [128, 768, 2048], P('ep', 'grp'), may hold values from -0.21875 to 0.21875
Outputs:
- grad_input: bfloat16 [32768, 2048], P(('grp', 'ep'))
- grad_gate: bfloat16 [128, 2048, 768], P('ep', None, 'grp')
- grad_up: bfloat16 [128, 2048, 768], P('ep', None, 'grp')
- grad_down: bfloat16 [128, 768, 2048], P('ep', 'grp')
The draws below stay inside these ranges and needn't reach their ends.
Inputs may be any that keep to these rules, and one draw needn't show every extreme that they name: `expert_ids`: each token names 4 different experts. Among the 128 tokens of one device no expert is named by more than 5 pairs, a bound that some block reaches.
All inputs are finite; a program needn't handle non-finite values.
Results may differ from the reference program's by a relative error of at most 0.012.
Values may be sent and summed in bfloat16 or wider, within the bound.
No kernel may reach another device: no remote copies, remote signals or barrier semaphores. Data moves between devices by JAX's collectives and lax.ppermute only.
A program may use at most 192 MiB of HBM per device.

```python
import math
import jax
import jax.numpy as jnp
import numpy as np
from jax import lax

D = 2048
HID = 768
TOP = 4
TOK_DEV = 128
EXPERTS = 128
CAP = 5
TOKENS = 32768


def block_scale(key, shape, pieces, smallest, largest):
    def one(position, blocks):
        heights = jax.random.uniform(jax.random.fold_in(jax.random.fold_in(key, 6), position), (blocks,), jnp.float32, smallest / len(pieces), largest / len(pieces))
        return jnp.repeat(jnp.exp(heights), shape[position] // blocks).reshape((-1,) + (1,) * (len(shape) - position - 1))

    gain = one(*pieces[0])
    for cut in pieces[1:]:
        gain = gain * one(*cut)
    return gain


def shared_out(key, own, number, rows, amount, top, bound, slope):
    ranking = jax.random.permutation(key, amount)
    packed, usual = load_shares(amount, rows * top, bound, slope, True), load_shares(amount, rows * top, bound, slope, False)
    places = jnp.arange(amount)

    def named(sizes, offset_by):
        used = int((sizes > 0).sum())
        fixed = max(1, used // 4)
        passed = fixed + (places - fixed + offset_by * (used - fixed)) % max(1, amount - fixed)
        return jnp.zeros((amount,), jnp.int32).at[ranking[jnp.where(places < fixed, places, passed)]].set(jnp.asarray(sizes, jnp.int32))

    sizes = jnp.where(number % 4 == 0, named(packed, number // 4), named(usual, number - number // 4 - 1))
    mixed = jax.random.permutation(jax.random.fold_in(own, 3), amount)
    source_of, sink = mixed[0:amount // 2 * 2:2], mixed[1:amount // 2 * 2:2]
    room = jnp.minimum(sizes[source_of] - 1, bound - sizes[sink]) // 2
    room = jnp.where((source_of == ranking[0]) | (sink == ranking[0]) | (sizes[sink] == 0), 0, jnp.maximum(room, 0))
    passed = jax.random.randint(jax.random.fold_in(own, 4), (amount // 2,), 0, 1 << 20) % (room + 1)
    sizes = sizes.at[source_of].add(-passed).at[sink].add(passed)
    members = jnp.searchsorted(jnp.cumsum(sizes), jnp.arange(rows * top), side="right").astype(jnp.int32)
    listing = members.reshape(top, rows).T
    listing = listing[jax.random.permutation(jax.random.fold_in(own, 1), rows)]
    offset_by = jax.random.randint(jax.random.fold_in(own, 2), (rows, 1), 0, top)
    return jnp.take_along_axis(listing, (jnp.arange(top)[None, :] + offset_by) % top, axis=1)


def load_shares(number_of, total, bound, skew, full):
    loads = [(1 << 20) // math.isqrt(rank ** skew) + 1 for rank in range(1, number_of + 1)]
    largest = bound if full else min(bound, max(-(-total // number_of), total * loads[0] // sum(loads)))
    least = 1 if total - largest >= number_of - 1 else 0
    holding, rest = [largest] + [least] * (number_of - 1), total - largest - least * (number_of - 1)
    while rest > 0:
        movable = [i for i in range(1, number_of) if holding[i] < largest] or [i for i in range(1, number_of) if holding[i] < bound]
        pool, remaining = sum([loads[i] for i in movable]), rest
        for i in movable:
            extra = min(bound - holding[i], max(1, remaining * loads[i] // pool), rest)
            holding[i] = holding[i] + extra
            rest = rest - extra
    return np.array(holding)


def bell_draw(rng, dims, spread, limit, pieces=(), held_as=jnp.bfloat16):
    result = spread * jax.random.normal(rng, dims, jnp.float32)
    if pieces:
        result = result * block_scale(rng, dims, pieces, -0.22, 0.18)
    return jnp.clip(result, -limit, limit).astype(held_as)


def setup_inputs(seed: int = 0) -> dict:
    key_list = jax.random.split(jax.random.key(seed), 8)
    activations = bell_draw(key_list[0], (TOKENS, D), 1.0, 6.0, ((0, 256),))
    out_grad = bell_draw(key_list[1], (TOKENS, D), 0.5, 6.0, ((0, 256),))
    expert_ids_keys = jax.random.split(jax.random.fold_in(key_list[2], 1), TOKENS // TOK_DEV)
    expert_ids_turns = jax.random.permutation(jax.random.fold_in(key_list[2], 3), TOKENS // TOK_DEV)
    expert_ids = jax.vmap(lambda own, number: shared_out(jax.random.fold_in(key_list[2], 2), own, number, TOK_DEV, EXPERTS, TOP, CAP, 2))(expert_ids_keys, expert_ids_turns).reshape((TOKENS, TOP))
    gate_values = jnp.clip(jnp.exp(math.log(1.0) - 2.9996462 * jax.random.uniform(key_list[3], (TOKENS, TOP), jnp.float32) ** block_scale(key_list[3], (TOKENS, TOP), ((0, 256),), -0.2, 0.2)), 0.049804688, 1.0).astype(jnp.bfloat16)
    w_gate = bell_draw(key_list[4], (EXPERTS, D, HID), D ** -0.5, 0.125, ((0, 128), (2, 2)))
    w_up = bell_draw(key_list[5], (EXPERTS, D, HID), D ** -0.5, 0.125, ((0, 128), (2, 2)))
    w_down = bell_draw(key_list[6], (EXPERTS, HID, D), HID ** -0.5, 0.21875, ((0, 128), (1, 2)))
    return {"activations": activations, "out_grad": out_grad, "expert_ids": expert_ids, "gate_values": gate_values, "w_gate": w_gate, "w_up": w_up, "w_down": w_down}


def routing_table(expert_ids, experts, capacity):
    flattened = expert_ids.reshape(-1).astype(jnp.int32)
    onehot = (flattened[:, None] == jnp.arange(experts, dtype=jnp.int32)[None, :]).astype(jnp.int32)
    earlier = (jnp.cumsum(onehot, axis=0) - onehot).astype(jnp.int32)
    slot_index = jnp.sum(earlier * onehot, axis=1).astype(jnp.int32)
    source_table = jnp.full((experts, capacity), -1, jnp.int32)
    source_table = source_table.at[flattened, slot_index].set(jnp.arange(flattened.shape[0], dtype=jnp.int32))
    return slot_index, source_table


def contract_rows(left, right):
    return lax.dot_general(left, right, (((0,), (0,)), ((), ())), preferred_element_type=jnp.float32)


def contract_last(left, right):
    return lax.dot_general(left, right, (((1,), (1,)), ((), ())), preferred_element_type=jnp.float32)


def expert_backward(token_rows, upstream_rows, gate_rows, gate_weight, up_weight, down_weight):
    pre_gate = jnp.dot(token_rows, gate_weight, preferred_element_type=jnp.float32)
    pre_up = jnp.dot(token_rows, up_weight, preferred_element_type=jnp.float32)
    sigmoid_gate = jax.nn.sigmoid(pre_gate)
    silu_gate = pre_gate * sigmoid_gate
    row_scale = gate_rows.astype(jnp.float32)[:, None]
    weighted = (row_scale * silu_gate * pre_up).astype(jnp.bfloat16)
    grad_down = contract_rows(weighted, upstream_rows)
    grad_hidden = row_scale * contract_last(upstream_rows, down_weight)
    grad_pre_gate = (grad_hidden * pre_up * sigmoid_gate * (1.0 + pre_gate * (1.0 - sigmoid_gate))).astype(jnp.bfloat16)
    grad_pre_up = (grad_hidden * silu_gate).astype(jnp.bfloat16)
    grad_gate = contract_rows(token_rows, grad_pre_gate)
    grad_up = contract_rows(token_rows, grad_pre_up)
    return grad_pre_gate, grad_pre_up, grad_gate, grad_up, grad_down


def input_rows(grad_pre_gate, grad_pre_up, gate_weight, up_weight):
    return contract_last(grad_pre_gate, gate_weight) + contract_last(grad_pre_up, up_weight)


def reference(activations, out_grad, expert_ids, gate_values, w_gate, w_up, w_down):
    blocks = TOKENS // TOK_DEV
    pair_count = TOK_DEV * TOP
    id_blocks = expert_ids.reshape(blocks, TOK_DEV, TOP)
    tables = jax.vmap(lambda block_ids: routing_table(block_ids, EXPERTS, CAP)[1])(id_blocks)
    offsets = (jnp.arange(blocks, dtype=jnp.int32) * pair_count)[:, None, None]
    shifted = jnp.where(tables >= 0, tables + offsets, -1).astype(jnp.int32)
    per_expert = jnp.transpose(shifted, (1, 0, 2)).reshape(EXPERTS, blocks * CAP)
    flat_gates = gate_values.reshape(-1)
    zero_value = jnp.zeros((), jnp.bfloat16)

    def expert_step(running, inputs):
        gate_weight, up_weight, down_weight, sources = inputs
        occupied = sources >= 0
        safe_index = jnp.where(occupied, sources, 0).astype(jnp.int32)
        token_index = (safe_index // TOP).astype(jnp.int32)
        token_rows = jnp.where(occupied[:, None], activations[token_index], zero_value)
        upstream_rows = jnp.where(occupied[:, None], out_grad[token_index], zero_value)
        gate_rows = jnp.where(occupied, flat_gates[safe_index], zero_value)
        grad_pre_gate, grad_pre_up, grad_gate, grad_up, grad_down = expert_backward(
            token_rows, upstream_rows, gate_rows, gate_weight, up_weight, down_weight)
        rounded = lax.optimization_barrier(input_rows(grad_pre_gate, grad_pre_up, gate_weight, up_weight).astype(jnp.bfloat16))
        target = jnp.where(occupied, token_index, TOKENS).astype(jnp.int32)
        running = running.at[target].add(rounded.astype(jnp.float32), mode="drop")
        return running, (grad_gate.astype(jnp.bfloat16), grad_up.astype(jnp.bfloat16), grad_down.astype(jnp.bfloat16))

    initial = jnp.zeros((TOKENS, D), jnp.float32)
    accumulated, grads = lax.scan(expert_step, initial, (w_gate, w_up, w_down, per_expert))
    return accumulated.astype(jnp.bfloat16), grads[0], grads[1], grads[2]
```

```python
import jax
import jax.numpy as jnp
from jax import lax
from jax.experimental import pallas as pl
from jax.experimental.pallas import tpu as pltpu
from jax.sharding import PartitionSpec as P

CAP = 5
VMEM = pl.BlockSpec(memory_space=pltpu.VMEM)
SMEM = pl.BlockSpec(memory_space=pltpu.SMEM)


def slot_kernel(ids, gates, x, dy, send_x, send_dy, place, count):
    tokens, experts = x.shape[0], count.shape[0]

    def clear_count(e, carry):
        count[e] = 0
        return carry

    lax.fori_loop(0, experts, clear_count, 0, unroll=8)
    send_x[...] = jnp.zeros_like(send_x)
    send_dy[...] = jnp.zeros_like(send_dy)

    def one_token(t, carry):
        x_row = x[t]
        dy_row = dy[t].astype(jnp.float32)
        for k in range(4):
            pair = t * 4 + k
            expert = ids[pair]
            taken = count[expert]
            count[expert] = taken + 1
            slot = expert * CAP + taken
            place[pair] = slot
            send_x[slot] = x_row
            send_dy[slot] = (dy_row * gates[pair]).astype(jnp.bfloat16)
        return carry

    lax.fori_loop(0, tokens, one_token, 0, unroll=2)


def fill_slots(ids, gates, x, dy, experts):
    rows = experts * CAP
    out = jax.ShapeDtypeStruct((rows,) + x.shape[1:], jnp.bfloat16)
    return pl.pallas_call(
        slot_kernel,
        out_shape=(out, out, jax.ShapeDtypeStruct(ids.shape, jnp.int32)),
        in_specs=[SMEM, SMEM, VMEM, VMEM],
        out_specs=(VMEM, VMEM, SMEM),
        scratch_shapes=[pltpu.SMEM((experts,), jnp.int32)],
        compiler_params=pltpu.CompilerParams(vmem_limit_bytes=32 * 2**20),
        name="fill_slots",
    )(ids, gates, x, dy)


def combine_kernel(place, rows, out):
    def one_token(t, carry):
        total = rows[place[4 * t]].astype(jnp.float32)
        for k in range(1, 4):
            total = total + rows[place[4 * t + k]].astype(jnp.float32)
        out[t] = total.astype(jnp.bfloat16)
        return carry

    lax.fori_loop(0, out.shape[0], one_token, 0, unroll=2)


def combine(place, rows, tokens):
    return pl.pallas_call(
        combine_kernel,
        out_shape=jax.ShapeDtypeStruct((tokens,) + rows.shape[1:], jnp.bfloat16),
        in_specs=[SMEM, VMEM],
        out_specs=VMEM,
        compiler_params=pltpu.CompilerParams(vmem_limit_bytes=32 * 2**20),
        name="combine",
    )(place, rows)


def contract(left, right, dims):
    return lax.dot_general(left, right, (dims, ((), ())), preferred_element_type=jnp.float32)


def local(activations, out_grad, expert_ids, gate_values, w_gate, w_up, w_down):
    experts = lax.axis_size("ep")
    tokens, width = activations.shape
    lanes = (width // 128, 128)
    swap = lambda a: lax.ppermute(a, "grp", [(0, 1), (1, 0)])
    exchange = lambda a: lax.all_to_all(a, "ep", split_axis=0, concat_axis=0, tiled=True)

    send_x, send_dy, place = fill_slots(
        expert_ids.reshape(-1),
        gate_values.reshape(-1).astype(jnp.float32),
        activations.reshape((tokens,) + lanes),
        out_grad.reshape((tokens,) + lanes),
        experts,
    )
    gate_w = jnp.concatenate([w_gate[0], swap(w_gate[0])], axis=1)
    up_w = jnp.concatenate([w_up[0], swap(w_up[0])], axis=1)
    down_w = jnp.concatenate([w_down[0], swap(w_down[0])], axis=0)

    x = exchange(send_x).reshape(-1, width)
    pre_gate = contract(x, gate_w, ((1,), (0,)))
    pre_up = contract(x, up_w, ((1,), (0,)))
    sig = jax.nn.sigmoid(pre_gate)
    silu = pre_gate * sig
    weighted = (silu * pre_up).astype(jnp.bfloat16)

    dy = exchange(send_dy).reshape(-1, width)
    grad_hidden = contract(dy, down_w, ((1,), (1,)))
    grad_pre_gate = (grad_hidden * pre_up * sig * (1.0 + pre_gate * (1.0 - sig))).astype(jnp.bfloat16)
    grad_pre_up = (grad_hidden * silu).astype(jnp.bfloat16)
    row_grad = (
        contract(grad_pre_gate, gate_w, ((1,), (1,))) + contract(grad_pre_up, up_w, ((1,), (1,)))
    ).astype(jnp.bfloat16)
    returned = exchange(row_grad.reshape((-1,) + lanes))

    half = w_gate.shape[2]
    rows_t = ((0,), (0,))
    theirs = swap(
        (
            contract(x, grad_pre_gate[:, half:], rows_t).astype(jnp.bfloat16),
            contract(x, grad_pre_up[:, half:], rows_t).astype(jnp.bfloat16),
            contract(weighted[:, half:], dy, rows_t).astype(jnp.bfloat16),
        )
    )
    mine = (
        contract(x, grad_pre_gate[:, :half], rows_t),
        contract(x, grad_pre_up[:, :half], rows_t),
        contract(weighted[:, :half], dy, rows_t),
    )
    grads = [(m + t.astype(jnp.float32)).astype(jnp.bfloat16)[None] for m, t in zip(mine, theirs)]
    grad_input = combine(place, returned, tokens).reshape(tokens, width)
    return (grad_input, *grads)


def solution(mesh):
    tokens = P(("grp", "ep"), None)
    columns, rows = P("ep", None, "grp"), P("ep", "grp", None)
    return jax.shard_map(
        local,
        mesh=mesh,
        in_specs=(tokens, tokens, tokens, tokens, columns, columns, rows),
        out_specs=(tokens, columns, columns, rows),
        check_vma=False,
    )
```

```python
import functools

import jax
import jax.numpy as jnp
from jax import lax
from jax.experimental import pallas as pl
from jax.experimental.pallas import tpu as pltpu
from jax.sharding import PartitionSpec as P

CAP = 5
VMEM = pl.BlockSpec(memory_space=pltpu.VMEM)
SMEM = pl.BlockSpec(memory_space=pltpu.SMEM)


def fill_x_kernel(ids, x, send_x, place, count):
    top, tokens = ids.shape

    def clear_count(e, carry):
        count[e] = 0
        return carry

    lax.fori_loop(0, count.shape[0], clear_count, 0, unroll=8)
    send_x[...] = jnp.zeros_like(send_x)

    def one_token(t, carry):
        row = x[t]
        for k in range(top):
            expert = ids[k, t]
            taken = count[expert]
            count[expert] = taken + 1
            slot = expert * CAP + taken
            place[k, t] = slot
            send_x[slot] = row
        return carry

    lax.fori_loop(0, tokens, one_token, 0, unroll=2)


def fill_dy_kernel(place, gates, dy, send_dy):
    top, tokens = place.shape
    send_dy[...] = jnp.zeros_like(send_dy)

    def one_token(t, carry):
        row = dy[t].astype(jnp.float32)
        for k in range(top):
            send_dy[place[k, t]] = (row * gates[k, t]).astype(jnp.bfloat16)
        return carry

    lax.fori_loop(0, tokens, one_token, 0, unroll=2)


def fill_x(ids, x, experts):
    return pl.pallas_call(
        fill_x_kernel,
        out_shape=(
            jax.ShapeDtypeStruct((experts * CAP,) + x.shape[1:], x.dtype),
            jax.ShapeDtypeStruct(ids.shape, jnp.int32),
        ),
        in_specs=[SMEM, VMEM],
        out_specs=(VMEM, SMEM),
        scratch_shapes=[pltpu.SMEM((experts,), jnp.int32)],
        compiler_params=pltpu.CompilerParams(vmem_limit_bytes=16 * 2**20),
        name="fill_x",
    )(ids, x)


def fill_dy(place, gates, dy, experts):
    return pl.pallas_call(
        fill_dy_kernel,
        out_shape=jax.ShapeDtypeStruct((experts * CAP,) + dy.shape[1:], dy.dtype),
        in_specs=[SMEM, SMEM, VMEM],
        out_specs=VMEM,
        compiler_params=pltpu.CompilerParams(vmem_limit_bytes=16 * 2**20),
        cost_estimate=pl.CostEstimate(flops=10**7, bytes_accessed=8 * 2**20, transcendentals=0),
        name="fill_dy",
    )(place, gates, dy)


def row_grads_kernel(parts, columns, dy, slope, silu, w_down, w_gate, w_up, out, grad_gate, grad_up):
    rows, blocks, lanes = dy.shape
    width = blocks * lanes
    step, group = rows // parts, blocks // columns
    for i in range(parts):
        r = pl.ds(i * step, step)
        grad_hidden = contract(dy[r].reshape(step, width), w_down[...], ((1,), (1,)))
        grad_gate[r, :] = (grad_hidden * slope[r, :]).astype(jnp.bfloat16)
        grad_up[r, :] = (grad_hidden * silu[r, :]).astype(jnp.bfloat16)
        for c in range(columns):
            w = pl.ds(c * group * lanes, group * lanes)
            total = contract(grad_gate[r, :], w_gate[w, :], ((1,), (1,)))
            total = total + contract(grad_up[r, :], w_up[w, :], ((1,), (1,)))
            out[r, pl.ds(c * group, group), :] = total.astype(jnp.bfloat16).reshape(step, group, lanes)


def row_grads(dy, slope, silu, w_down, w_gate, w_up):
    rows, hidden = slope.shape
    part = jax.ShapeDtypeStruct((rows, hidden), jnp.bfloat16)
    return pl.pallas_call(
        functools.partial(row_grads_kernel, 2, 4),
        out_shape=(jax.ShapeDtypeStruct(dy.shape, jnp.bfloat16), part, part),
        in_specs=[VMEM] * 6,
        out_specs=(VMEM,) * 3,
        compiler_params=pltpu.CompilerParams(vmem_limit_bytes=28 * 2**20),
        cost_estimate=pl.CostEstimate(
            flops=6 * rows * w_gate.size, bytes_accessed=8 * 2**20, transcendentals=0
        ),
        name="row_grads",
    )(dy, slope, silu, w_down, w_gate, w_up)


def combine_kernel(place, rows, out):
    def one_token(t, carry):
        total = rows[place[0, t]].astype(jnp.float32)
        for k in range(1, place.shape[0]):
            total = total + rows[place[k, t]].astype(jnp.float32)
        out[t] = total.astype(jnp.bfloat16)
        return carry

    lax.fori_loop(0, out.shape[0], one_token, 0, unroll=2)


def combine(place, rows, tokens):
    return pl.pallas_call(
        combine_kernel,
        out_shape=jax.ShapeDtypeStruct((tokens,) + rows.shape[1:], jnp.bfloat16),
        in_specs=[SMEM, VMEM],
        out_specs=VMEM,
        compiler_params=pltpu.CompilerParams(vmem_limit_bytes=16 * 2**20),
        name="combine",
    )(place, rows)


def contract(left, right, dims):
    return lax.dot_general(left, right, (dims, ((), ())), preferred_element_type=jnp.float32)


def local(activations, out_grad, expert_ids, gate_values, w_gate, w_up, w_down):
    experts = lax.axis_size("ep")
    tokens, width = activations.shape
    lanes = (width // 128, 128)
    swap = lambda a: lax.ppermute(a, "grp", [(0, 1), (1, 0)])
    exchange = lambda a: lax.all_to_all(a, "ep", split_axis=0, concat_axis=0, tiled=True)

    send_x, place = fill_x(expert_ids.T, activations.reshape((tokens,) + lanes), experts)
    send_dy = fill_dy(
        place, gate_values.T.astype(jnp.float32), out_grad.reshape((tokens,) + lanes), experts
    )
    gate_w = jnp.concatenate([w_gate[0], swap(w_gate[0])], axis=1)
    up_w = jnp.concatenate([w_up[0], swap(w_up[0])], axis=1)
    down_w = jnp.concatenate([w_down[0], swap(w_down[0])], axis=0)

    arrived_x, send_dy = lax.optimization_barrier((exchange(send_x), send_dy))
    x = arrived_x.reshape(-1, width)
    pre_gate = contract(x, gate_w, ((1,), (0,)))
    pre_up = contract(x, up_w, ((1,), (0,)))
    sig = jax.nn.sigmoid(pre_gate)
    silu = pre_gate * sig
    slope = pre_up * sig * (1.0 + pre_gate * (1.0 - sig))
    weighted = (silu * pre_up).astype(jnp.bfloat16)
    slope, silu, weighted = lax.optimization_barrier((slope, silu, weighted))

    arrived_dy = exchange(send_dy)
    row_grad, grad_pre_gate, grad_pre_up = row_grads(arrived_dy, slope, silu, down_w, gate_w, up_w)
    returned = exchange(row_grad)

    half = w_gate.shape[2]
    dy = arrived_dy.reshape(-1, width)
    rows_t = ((0,), (0,))
    theirs = swap(
        (
            contract(x, grad_pre_gate[:, half:], rows_t).astype(jnp.bfloat16),
            contract(x, grad_pre_up[:, half:], rows_t).astype(jnp.bfloat16),
            contract(weighted[:, half:], dy, rows_t).astype(jnp.bfloat16),
        )
    )
    mine = (
        contract(x, grad_pre_gate[:, :half], rows_t),
        contract(x, grad_pre_up[:, :half], rows_t),
        contract(weighted[:, :half], dy, rows_t),
    )
    grads = [(m + t.astype(jnp.float32)).astype(jnp.bfloat16)[None] for m, t in zip(mine, theirs)]
    grad_input = combine(place, returned, tokens).reshape(tokens, width)
    return (grad_input, *grads)


def solution(mesh):
    tokens = P(("grp", "ep"), None)
    columns, rows = P("ep", None, "grp"), P("ep", "grp", None)
    return jax.shard_map(
        local,
        mesh=mesh,
        in_specs=(tokens, tokens, tokens, tokens, columns, columns, rows),
        out_specs=(tokens, columns, columns, rows),
        check_vma=False,
    )
```

```python
import functools

import jax
import jax.numpy as jnp
from jax import lax
from jax.experimental import pallas as pl
from jax.experimental.pallas import tpu as pltpu
from jax.sharding import PartitionSpec as P

CAP = 5
VMEM = pl.BlockSpec(memory_space=pltpu.VMEM)
ANY = pl.BlockSpec(memory_space=pl.ANY)
SMEM = pl.BlockSpec(memory_space=pltpu.SMEM)


def fill_kernel(ids, gates, x, dy, out, place, send, count, sem):
    top, tokens = ids.shape

    def clear_count(e, carry):
        count[e] = 0
        return carry

    lax.fori_loop(0, count.shape[0], clear_count, 0, unroll=8)
    send[...] = jnp.zeros_like(send)

    def one_token(t, carry):
        x_row = x[t]
        dy_row = dy[t].astype(jnp.float32)
        for k in range(top):
            expert = ids[k, t]
            taken = count[expert]
            count[expert] = taken + 1
            place[k, t] = expert * CAP + taken
            slot = expert * (2 * CAP) + taken
            send[slot] = x_row
            send[slot + CAP] = (dy_row * gates[k, t]).astype(jnp.bfloat16)
        return carry

    lax.fori_loop(0, tokens, one_token, 0, unroll=4)
    done = pltpu.make_async_copy(send, out, sem)
    done.start()
    done.wait()


def fill_slots(ids, gates, x, dy, experts):
    shape = (experts * 2 * CAP,) + x.shape[1:]
    return pl.pallas_call(
        fill_kernel,
        out_shape=(jax.ShapeDtypeStruct(shape, x.dtype), jax.ShapeDtypeStruct(ids.shape, jnp.int32)),
        in_specs=[SMEM, SMEM, VMEM, VMEM],
        out_specs=(ANY, SMEM),
        scratch_shapes=[
            pltpu.VMEM(shape, x.dtype),
            pltpu.SMEM((experts,), jnp.int32),
            pltpu.SemaphoreType.DMA,
        ],
        compiler_params=pltpu.CompilerParams(vmem_limit_bytes=58 * 2**20),
        name="fill_slots",
    )(ids, gates, x, dy)


def row_grads_kernel(
    parts, columns, arrived, gate_a, gate_b, up_a, up_b, down_a, down_b,
    out, weighted, grad_gate, grad_up,
    v_x, v_dy, v_gate, v_up, v_down, v_out, v_weighted, v_grad_gate, v_grad_up,
    x_sem, dy_sem, w_sem, out_sem,
):
    sources, _, blocks, lanes = arrived.shape
    half, width = down_a.shape
    some = sources // parts
    step, group = some * CAP, blocks // columns
    copy = pltpu.make_async_copy
    sides = (pl.ds(0, half), pl.ds(half, half))
    x_in, dy_in = [], []
    for i in range(parts):
        s = pl.ds(i * some, some)
        x_in.append(copy(arrived.at[s, pl.ds(0, CAP)], v_x.at[s], x_sem.at[i]))
        dy_in.append(copy(arrived.at[s, pl.ds(CAP, CAP)], v_dy.at[s], dy_sem.at[i]))
    gate_in = [copy(w, v_gate.at[:, d], w_sem.at[0 + j]) for j, (w, d) in enumerate(zip((gate_a, gate_b), sides))]
    up_in = [copy(w, v_up.at[:, d], w_sem.at[2 + j]) for j, (w, d) in enumerate(zip((up_a, up_b), sides))]
    down_in = [copy(w, v_down.at[d], w_sem.at[4 + j]) for j, (w, d) in enumerate(zip((down_a, down_b), sides))]
    for c in [x_in[0], *gate_in, *up_in, dy_in[0], *down_in]:
        c.start()
    for i in range(1, parts):
        x_in[i].start()
        dy_in[i].start()

    outs = []
    for i in range(parts):
        s, r = pl.ds(i * some, some), pl.ds(i * step, step)
        x_in[i].wait()
        x = v_x[s].reshape(step, width)
        if i == 0:
            for c in gate_in:
                c.wait()
        pre_gate = contract(x, v_gate[...], ((1,), (0,)))
        if i == 0:
            for c in up_in:
                c.wait()
        pre_up = contract(x, v_up[...], ((1,), (0,)))
        sig = jax.nn.sigmoid(pre_gate)
        silu = pre_gate * sig
        v_weighted[r, :] = (silu * pre_up).astype(jnp.bfloat16)
        dy_in[i].wait()
        if i == 0:
            for c in down_in:
                c.wait()
        grad_hidden = contract(v_dy[s].reshape(step, width), v_down[...], ((1,), (1,)))
        slope = pre_up * sig * (1.0 + pre_gate * (1.0 - sig))
        v_grad_gate[r, :] = (grad_hidden * slope).astype(jnp.bfloat16)
        v_grad_up[r, :] = (grad_hidden * silu).astype(jnp.bfloat16)
        for c in range(columns):
            w = pl.ds(c * group * lanes, group * lanes)
            total = contract(v_grad_gate[r, :], v_gate[w, :], ((1,), (1,)))
            total = total + contract(v_grad_up[r, :], v_up[w, :], ((1,), (1,)))
            v_out[r, pl.ds(c * group, group), :] = total.astype(jnp.bfloat16).reshape(step, group, lanes)
        pairs = ((v_out, out), (v_weighted, weighted), (v_grad_gate, grad_gate), (v_grad_up, grad_up))
        for j, (v, o) in enumerate(pairs):
            outs.append(copy(v.at[r], o.at[r], out_sem.at[4 * i + j]))
            outs[-1].start()
    for c in outs:
        c.wait()


def row_grads(arrived, gate_a, gate_b, up_a, up_b, down_a, down_b, parts=2, columns=2):
    sources, _, blocks, lanes = arrived.shape
    half, width = down_a.shape
    rows, hidden = sources * CAP, 2 * half
    struct = lambda *shape: jax.ShapeDtypeStruct(shape, jnp.bfloat16)
    vmem = lambda *shape: pltpu.VMEM(shape, jnp.bfloat16)
    dma = lambda n: pltpu.SemaphoreType.DMA((n,))
    return pl.pallas_call(
        functools.partial(row_grads_kernel, parts, columns),
        out_shape=(struct(rows, blocks, lanes),) + (struct(rows, hidden),) * 3,
        in_specs=[ANY] * 7,
        out_specs=(ANY,) * 4,
        scratch_shapes=[
            vmem(sources, CAP, blocks, lanes), vmem(sources, CAP, blocks, lanes),
            vmem(width, hidden), vmem(width, hidden), vmem(hidden, width),
            vmem(rows, blocks, lanes), vmem(rows, hidden), vmem(rows, hidden), vmem(rows, hidden),
            dma(parts), dma(parts), dma(6), dma(4 * parts),
        ],
        compiler_params=pltpu.CompilerParams(vmem_limit_bytes=58 * 2**20),
        cost_estimate=pl.CostEstimate(
            flops=10 * rows * hidden * width, bytes_accessed=24 * 2**20, transcendentals=rows * hidden
        ),
        name="row_grads",
    )(arrived, gate_a, gate_b, up_a, up_b, down_a, down_b)


def combine_kernel(place, rows, out):
    def one_token(t, carry):
        total = rows[place[0, t]].astype(jnp.float32)
        for k in range(1, place.shape[0]):
            total = total + rows[place[k, t]].astype(jnp.float32)
        out[t] = total.astype(jnp.bfloat16)
        return carry

    lax.fori_loop(0, out.shape[0], one_token, 0, unroll=2)


def combine(place, rows, tokens):
    return pl.pallas_call(
        combine_kernel,
        out_shape=jax.ShapeDtypeStruct((tokens,) + rows.shape[1:], jnp.bfloat16),
        in_specs=[SMEM, VMEM],
        out_specs=VMEM,
        compiler_params=pltpu.CompilerParams(vmem_limit_bytes=16 * 2**20),
        name="combine",
    )(place, rows)


def contract(left, right, dims):
    return lax.dot_general(left, right, (dims, ((), ())), preferred_element_type=jnp.float32)


def local(activations, out_grad, expert_ids, gate_values, w_gate, w_up, w_down):
    experts = lax.axis_size("ep")
    tokens, width = activations.shape
    lanes = (width // 128, 128)
    swap = lambda a: lax.ppermute(a, "grp", [(0, 1), (1, 0)])
    exchange = lambda a: lax.all_to_all(a, "ep", split_axis=0, concat_axis=0, tiled=True)

    send, place = fill_slots(
        expert_ids.T,
        gate_values.T.astype(jnp.float32),
        activations.reshape((tokens,) + lanes),
        out_grad.reshape((tokens,) + lanes),
        experts,
    )
    weights = []
    for w in (w_gate[0], w_up[0], w_down[0]):
        weights += [w, swap(w)]
    arrived = exchange(send).reshape((experts, 2 * CAP) + lanes)
    row_grad, weighted, grad_pre_gate, grad_pre_up = row_grads(arrived, *weights)
    returned = exchange(row_grad)

    half = w_gate.shape[2]
    x, dy = (arrived[:, i * CAP : (i + 1) * CAP].reshape(-1, width) for i in range(2))
    rows_t = ((0,), (0,))
    theirs = swap(
        (
            contract(x, grad_pre_gate[:, half:], rows_t).astype(jnp.bfloat16),
            contract(x, grad_pre_up[:, half:], rows_t).astype(jnp.bfloat16),
            contract(weighted[:, half:], dy, rows_t).astype(jnp.bfloat16),
        )
    )
    mine = (
        contract(x, grad_pre_gate[:, :half], rows_t),
        contract(x, grad_pre_up[:, :half], rows_t),
        contract(weighted[:, :half], dy, rows_t),
    )
    grads = [(m + t.astype(jnp.float32)).astype(jnp.bfloat16)[None] for m, t in zip(mine, theirs)]
    grad_input = combine(place, returned, tokens).reshape(tokens, width)
    return (grad_input, *grads)


def solution(mesh):
    tokens = P(("grp", "ep"), None)
    columns, rows = P("ep", None, "grp"), P("ep", "grp", None)
    return jax.shard_map(
        local,
        mesh=mesh,
        in_specs=(tokens, tokens, tokens, tokens, columns, columns, rows),
        out_specs=(tokens, columns, columns, rows),
        check_vma=False,
    )
```

```python
import functools

import jax
import jax.numpy as jnp
from jax import lax
from jax.experimental import pallas as pl
from jax.experimental.pallas import tpu as pltpu
from jax.sharding import PartitionSpec as P

CAP = 5
VMEM = pl.BlockSpec(memory_space=pltpu.VMEM)
ANY = pl.BlockSpec(memory_space=pl.ANY)
SMEM = pl.BlockSpec(memory_space=pltpu.SMEM)


def fill_kernel(chunks, ids, gates, x, dy, out, place, v_x, v_dy, send, v_token, v_gate, token_of, gate_of, sems):
    top, tokens = ids.shape
    blocks, lanes = send.shape[1:]
    experts = send.shape[0] // (2 * CAP)
    f32, bf16 = jnp.float32, jnp.bfloat16
    expert_id = lax.broadcasted_iota(jnp.int32, (experts, tokens), 0)
    names = [expert_id == ids[k : k + 1, :] for k in range(top)]
    named = jnp.zeros((experts, tokens), f32)
    gate = jnp.zeros((experts, tokens), f32)
    for k in range(top):
        named = named + names[k].astype(f32)
        gate = gate + jnp.where(names[k], gates[k : k + 1, :].astype(f32), 0.0)
    before = lax.broadcasted_iota(jnp.int32, (tokens, tokens), 0) < lax.broadcasted_iota(jnp.int32, (tokens, tokens), 1)
    earlier = contract(named.astype(bf16), before.astype(f32).astype(bf16), ((1,), (0,)))
    for k in range(top):
        slot = jnp.sum(jnp.where(names[k], earlier, 0.0), axis=0, keepdims=True)
        place[k : k + 1, :] = ids[k : k + 1, :] * CAP + slot.astype(jnp.int32)
    number = lax.broadcasted_iota(jnp.int32, (8, tokens), 1).astype(f32).astype(bf16)
    ones = jnp.ones((8, tokens), bf16)
    last = ((1,), (1,))
    for c in range(CAP):
        holds = jnp.where(earlier == c, named, 0.0)
        full = contract(ones, holds.astype(bf16), last)[:1]
        token = contract(number, holds.astype(bf16), last)[:1]
        v_token[c : c + 1, :] = jnp.where(full > 0.5, token, float(tokens)).astype(jnp.int32)
        v_gate[c : c + 1, :] = contract(ones, (holds * gate).astype(bf16), last)[:1]
    tables = [
        pltpu.make_async_copy(v_token, token_of, sems.at[0]),
        pltpu.make_async_copy(v_gate, gate_of, sems.at[1]),
    ]
    for t in tables:
        t.start()
    for rows, v in ((x, v_x), (dy, v_dy)):
        v[pl.ds(0, tokens)] = rows[...].reshape(tokens, blocks, lanes)
        v[tokens] = jnp.zeros((blocks, lanes), bf16)
    for t in tables:
        t.wait()

    def one_expert(e, carry):
        for c in range(CAP):
            token, slot = token_of[c, e], e * (2 * CAP) + c
            send[slot] = v_x[token]
            send[slot + CAP] = (v_dy[token].astype(f32) * gate_of[c, e]).astype(bf16)
        return carry

    some = experts // chunks
    done = []
    for i in range(chunks):
        lax.fori_loop(i * some, (i + 1) * some, one_expert, 0, unroll=2)
        r = pl.ds(i * some * 2 * CAP, some * 2 * CAP)
        done.append(pltpu.make_async_copy(send.at[r], out.at[r], sems.at[2 + i]))
        done[-1].start()
    for d in done:
        d.wait()


def fill_slots(ids, gates, x, dy, experts, chunks=4):
    tokens, width = x.shape
    tile = (width // 128, 128)
    shape = (experts * 2 * CAP,) + tile
    vmem = lambda *shape: pltpu.VMEM(shape, x.dtype)
    return pl.pallas_call(
        functools.partial(fill_kernel, chunks),
        out_shape=(jax.ShapeDtypeStruct(shape, x.dtype), jax.ShapeDtypeStruct(ids.shape, jnp.int32)),
        in_specs=[VMEM] * 4,
        out_specs=(ANY, VMEM),
        scratch_shapes=[
            vmem(tokens + 1, *tile), vmem(tokens + 1, *tile), vmem(*shape),
            pltpu.VMEM((8, experts), jnp.int32), pltpu.VMEM((8, experts), jnp.float32),
            pltpu.SMEM((8, experts), jnp.int32), pltpu.SMEM((8, experts), jnp.float32),
            pltpu.SemaphoreType.DMA((2 + chunks,)),
        ],
        compiler_params=pltpu.CompilerParams(vmem_limit_bytes=58 * 2**20),
        name="fill_slots",
    )(ids, gates, x, dy)


def row_grads_kernel(
    parts, columns, arrived, gate_a, gate_b, up_a, up_b, down_a, down_b,
    out, weighted, grad_gate, grad_up,
    v_x, v_dy, v_gate, v_up, v_down, v_out, v_weighted, v_grad_gate, v_grad_up,
    x_sem, dy_sem, w_sem, out_sem,
):
    sources, _, blocks, lanes = arrived.shape
    half, width = down_a.shape
    some = sources // parts
    step, group = some * CAP, blocks // columns
    copy = pltpu.make_async_copy
    sides = (pl.ds(0, half), pl.ds(half, half))
    x_in, dy_in = [], []
    for i in range(parts):
        s = pl.ds(i * some, some)
        x_in.append(copy(arrived.at[s, pl.ds(0, CAP)], v_x.at[s], x_sem.at[i]))
        dy_in.append(copy(arrived.at[s, pl.ds(CAP, CAP)], v_dy.at[s], dy_sem.at[i]))
    gate_in = [copy(w, v_gate.at[:, d], w_sem.at[0 + j]) for j, (w, d) in enumerate(zip((gate_a, gate_b), sides))]
    up_in = [copy(w, v_up.at[:, d], w_sem.at[2 + j]) for j, (w, d) in enumerate(zip((up_a, up_b), sides))]
    down_in = [copy(w, v_down.at[d], w_sem.at[4 + j]) for j, (w, d) in enumerate(zip((down_a, down_b), sides))]
    for c in [x_in[0], *gate_in, *up_in, dy_in[0], *down_in]:
        c.start()
    for i in range(1, parts):
        x_in[i].start()
        dy_in[i].start()

    outs = []
    for i in range(parts):
        s, r = pl.ds(i * some, some), pl.ds(i * step, step)
        x_in[i].wait()
        x = v_x[s].reshape(step, width)
        if i == 0:
            for c in gate_in:
                c.wait()
        pre_gate = contract(x, v_gate[...], ((1,), (0,)))
        if i == 0:
            for c in up_in:
                c.wait()
        pre_up = contract(x, v_up[...], ((1,), (0,)))
        sig = jax.nn.sigmoid(pre_gate)
        silu = pre_gate * sig
        v_weighted[r, :] = (silu * pre_up).astype(jnp.bfloat16)
        dy_in[i].wait()
        if i == 0:
            for c in down_in:
                c.wait()
        grad_hidden = contract(v_dy[s].reshape(step, width), v_down[...], ((1,), (1,)))
        slope = pre_up * sig * (1.0 + pre_gate * (1.0 - sig))
        v_grad_gate[r, :] = (grad_hidden * slope).astype(jnp.bfloat16)
        v_grad_up[r, :] = (grad_hidden * silu).astype(jnp.bfloat16)
        for c in range(columns):
            w = pl.ds(c * group * lanes, group * lanes)
            total = contract(v_grad_gate[r, :], v_gate[w, :], ((1,), (1,)))
            total = total + contract(v_grad_up[r, :], v_up[w, :], ((1,), (1,)))
            v_out[r, pl.ds(c * group, group), :] = total.astype(jnp.bfloat16).reshape(step, group, lanes)
        pairs = ((v_out, out), (v_weighted, weighted), (v_grad_gate, grad_gate), (v_grad_up, grad_up))
        for j, (v, o) in enumerate(pairs):
            outs.append(copy(v.at[r], o.at[r], out_sem.at[4 * i + j]))
            outs[-1].start()
    for c in outs:
        c.wait()


def row_grads(arrived, gate_a, gate_b, up_a, up_b, down_a, down_b, parts=2, columns=2):
    sources, _, blocks, lanes = arrived.shape
    half, width = down_a.shape
    rows, hidden = sources * CAP, 2 * half
    struct = lambda *shape: jax.ShapeDtypeStruct(shape, jnp.bfloat16)
    vmem = lambda *shape: pltpu.VMEM(shape, jnp.bfloat16)
    dma = lambda n: pltpu.SemaphoreType.DMA((n,))
    return pl.pallas_call(
        functools.partial(row_grads_kernel, parts, columns),
        out_shape=(struct(rows, blocks, lanes),) + (struct(rows, hidden),) * 3,
        in_specs=[ANY] * 7,
        out_specs=(ANY,) * 4,
        scratch_shapes=[
            vmem(sources, CAP, blocks, lanes), vmem(sources, CAP, blocks, lanes),
            vmem(width, hidden), vmem(width, hidden), vmem(hidden, width),
            vmem(rows, blocks, lanes), vmem(rows, hidden), vmem(rows, hidden), vmem(rows, hidden),
            dma(parts), dma(parts), dma(6), dma(4 * parts),
        ],
        compiler_params=pltpu.CompilerParams(vmem_limit_bytes=58 * 2**20),
        cost_estimate=pl.CostEstimate(
            flops=10 * rows * hidden * width, bytes_accessed=24 * 2**20, transcendentals=rows * hidden
        ),
        name="row_grads",
    )(arrived, gate_a, gate_b, up_a, up_b, down_a, down_b)


def combine_kernel(place, rows, out):
    def one_token(t, carry):
        total = rows[place[0, t]].astype(jnp.float32)
        for k in range(1, place.shape[0]):
            total = total + rows[place[k, t]].astype(jnp.float32)
        out[t] = total.astype(jnp.bfloat16)
        return carry

    lax.fori_loop(0, out.shape[0], one_token, 0, unroll=2)


def combine(place, rows, tokens):
    return pl.pallas_call(
        combine_kernel,
        out_shape=jax.ShapeDtypeStruct((tokens,) + rows.shape[1:], jnp.bfloat16),
        in_specs=[SMEM, VMEM],
        out_specs=VMEM,
        compiler_params=pltpu.CompilerParams(vmem_limit_bytes=16 * 2**20),
        name="combine",
    )(place, rows)


def contract(left, right, dims):
    return lax.dot_general(left, right, (dims, ((), ())), preferred_element_type=jnp.float32)


def local(activations, out_grad, expert_ids, gate_values, w_gate, w_up, w_down):
    experts = lax.axis_size("ep")
    tokens, width = activations.shape
    lanes = (width // 128, 128)
    swap = lambda a: lax.ppermute(a, "grp", [(0, 1), (1, 0)])
    exchange = lambda a: lax.all_to_all(a, "ep", split_axis=0, concat_axis=0, tiled=True)

    send, place = fill_slots(
        expert_ids.T, gate_values.T, activations, out_grad, experts
    )
    weights = []
    for w in (w_gate[0], w_up[0], w_down[0]):
        weights += [w, swap(w)]
    arrived = exchange(send).reshape((experts, 2 * CAP) + lanes)
    row_grad, weighted, grad_pre_gate, grad_pre_up = row_grads(arrived, *weights)
    returned = exchange(row_grad)

    half = w_gate.shape[2]
    x, dy = (arrived[:, i * CAP : (i + 1) * CAP].reshape(-1, width) for i in range(2))
    rows_t = ((0,), (0,))
    theirs = swap(
        (
            contract(x, grad_pre_gate[:, half:], rows_t).astype(jnp.bfloat16),
            contract(x, grad_pre_up[:, half:], rows_t).astype(jnp.bfloat16),
            contract(weighted[:, half:], dy, rows_t).astype(jnp.bfloat16),
        )
    )
    mine = (
        contract(x, grad_pre_gate[:, :half], rows_t),
        contract(x, grad_pre_up[:, :half], rows_t),
        contract(weighted[:, :half], dy, rows_t),
    )
    grads = [(m + t.astype(jnp.float32)).astype(jnp.bfloat16)[None] for m, t in zip(mine, theirs)]
    grad_input = combine(place, returned, tokens).reshape(tokens, width)
    return (grad_input, *grads)


def solution(mesh):
    tokens = P(("grp", "ep"), None)
    columns, rows = P("ep", None, "grp"), P("ep", "grp", None)
    return jax.shard_map(
        local,
        mesh=mesh,
        in_specs=(tokens, tokens, tokens, tokens, columns, columns, rows),
        out_specs=(tokens, columns, columns, rows),
        check_vma=False,
    )
```

```python
import functools

import jax
import jax.numpy as jnp
from jax import lax
from jax.experimental import pallas as pl
from jax.experimental.pallas import tpu as pltpu
from jax.sharding import PartitionSpec as P

CAP = 5
VMEM = pl.BlockSpec(memory_space=pltpu.VMEM)
ANY = pl.BlockSpec(memory_space=pl.ANY)
SMEM = pl.BlockSpec(memory_space=pltpu.SMEM)


def fill_kernel(chunks, ids, gates, x, dy, out, place, v_x, v_dy, send, v_token, v_gate, token_of, gate_of, sems):
    top, tokens = ids.shape
    blocks, lanes = send.shape[1:]
    experts = send.shape[0] // (2 * CAP)
    f32, bf16 = jnp.float32, jnp.bfloat16
    expert_id = lax.broadcasted_iota(jnp.int32, (experts, tokens), 0)
    names = [expert_id == ids[k : k + 1, :] for k in range(top)]
    named = jnp.zeros((experts, tokens), f32)
    gate = jnp.zeros((experts, tokens), f32)
    for k in range(top):
        named = named + names[k].astype(f32)
        gate = gate + jnp.where(names[k], gates[k : k + 1, :].astype(f32), 0.0)
    before = lax.broadcasted_iota(jnp.int32, (tokens, tokens), 0) < lax.broadcasted_iota(jnp.int32, (tokens, tokens), 1)
    earlier = contract(named.astype(bf16), before.astype(f32).astype(bf16), ((1,), (0,)))
    for k in range(top):
        slot = jnp.sum(jnp.where(names[k], earlier, 0.0), axis=0, keepdims=True)
        place[k : k + 1, :] = ids[k : k + 1, :] * CAP + slot.astype(jnp.int32)
    number = lax.broadcasted_iota(jnp.int32, (8, tokens), 1).astype(f32).astype(bf16)
    ones = jnp.ones((8, tokens), bf16)
    last = ((1,), (1,))
    for c in range(CAP):
        holds = jnp.where(earlier == c, named, 0.0)
        full = contract(ones, holds.astype(bf16), last)[:1]
        token = contract(number, holds.astype(bf16), last)[:1]
        v_token[c : c + 1, :] = jnp.where(full > 0.5, token, float(tokens)).astype(jnp.int32)
        v_gate[c : c + 1, :] = contract(ones, (holds * gate).astype(bf16), last)[:1]
    tables = [
        pltpu.make_async_copy(v_token, token_of, sems.at[0]),
        pltpu.make_async_copy(v_gate, gate_of, sems.at[1]),
    ]
    for t in tables:
        t.start()
    for rows, v in ((x, v_x), (dy, v_dy)):
        v[pl.ds(0, tokens)] = rows[...].reshape(tokens, blocks, lanes)
        v[tokens] = jnp.zeros((blocks, lanes), bf16)
    for t in tables:
        t.wait()

    def one_expert(e, carry):
        for c in range(CAP):
            token, slot = token_of[c, e], e * (2 * CAP) + c
            send[slot] = v_x[token]
            send[slot + CAP] = (v_dy[token].astype(f32) * gate_of[c, e]).astype(bf16)
        return carry

    some = experts // chunks
    done = []
    for i in range(chunks):
        lax.fori_loop(i * some, (i + 1) * some, one_expert, 0, unroll=2)
        r = pl.ds(i * some * 2 * CAP, some * 2 * CAP)
        done.append(pltpu.make_async_copy(send.at[r], out.at[r], sems.at[2 + i]))
        done[-1].start()
    for d in done:
        d.wait()


def fill_slots(ids, gates, x, dy, experts, chunks=4):
    tokens, width = x.shape
    tile = (width // 128, 128)
    shape = (experts * 2 * CAP,) + tile
    vmem = lambda *shape: pltpu.VMEM(shape, x.dtype)
    return pl.pallas_call(
        functools.partial(fill_kernel, chunks),
        out_shape=(jax.ShapeDtypeStruct(shape, x.dtype), jax.ShapeDtypeStruct(ids.shape, jnp.int32)),
        in_specs=[VMEM] * 4,
        out_specs=(ANY, VMEM),
        scratch_shapes=[
            vmem(tokens + 1, *tile), vmem(tokens + 1, *tile), vmem(*shape),
            pltpu.VMEM((8, experts), jnp.int32), pltpu.VMEM((8, experts), jnp.float32),
            pltpu.SMEM((8, experts), jnp.int32), pltpu.SMEM((8, experts), jnp.float32),
            pltpu.SemaphoreType.DMA((2 + chunks,)),
        ],
        compiler_params=pltpu.CompilerParams(vmem_limit_bytes=58 * 2**20),
        name="fill_slots",
    )(ids, gates, x, dy)


def row_grads_kernel(
    parts, columns, arrived, w_gate, up, down, out, weighted, grad_gate, grad_up,
    w_up, w_down, v_x, v_dy, v_out, v_weighted, v_grad_gate, v_grad_up, w_sem, x_sem, dy_sem, out_sem,
):
    sources, _, blocks, lanes = arrived.shape
    width = w_down.shape[1]
    some = sources // parts
    step, group = some * CAP, blocks // columns
    copy = pltpu.make_async_copy
    x_in, dy_in = [], []
    for i in range(parts):
        s = pl.ds(i * some, some)
        x_in.append(copy(arrived.at[s, pl.ds(0, CAP)], v_x.at[s], x_sem.at[i]))
        dy_in.append(copy(arrived.at[s, pl.ds(CAP, CAP)], v_dy.at[s], dy_sem.at[i]))
    up_in, down_in = copy(up, w_up, w_sem.at[0]), copy(down, w_down, w_sem.at[1])
    for c in (x_in[0], up_in, dy_in[0], down_in):
        c.start()
    for i in range(1, parts):
        x_in[i].start()
        dy_in[i].start()

    outs = []
    for i in range(parts):
        s, r = pl.ds(i * some, some), pl.ds(i * step, step)
        x_in[i].wait()
        x = v_x[s].reshape(step, width)
        pre_gate = contract(x, w_gate[...], ((1,), (0,)))
        if i == 0:
            up_in.wait()
        pre_up = contract(x, w_up[...], ((1,), (0,)))
        sig = jax.nn.sigmoid(pre_gate)
        silu = pre_gate * sig
        v_weighted[r, :] = (silu * pre_up).astype(jnp.bfloat16)
        dy_in[i].wait()
        if i == 0:
            down_in.wait()
        grad_hidden = contract(v_dy[s].reshape(step, width), w_down[...], ((1,), (1,)))
        slope = pre_up * sig * (1.0 + pre_gate * (1.0 - sig))
        v_grad_gate[r, :] = (grad_hidden * slope).astype(jnp.bfloat16)
        v_grad_up[r, :] = (grad_hidden * silu).astype(jnp.bfloat16)
        for c in range(columns):
            w = pl.ds(c * group * lanes, group * lanes)
            total = contract(v_grad_gate[r, :], w_gate[w, :], ((1,), (1,)))
            total = total + contract(v_grad_up[r, :], w_up[w, :], ((1,), (1,)))
            v_out[r, pl.ds(c * group, group), :] = total.astype(jnp.bfloat16).reshape(step, group, lanes)
        pairs = ((v_out, out), (v_weighted, weighted), (v_grad_gate, grad_gate), (v_grad_up, grad_up))
        for j, (v, o) in enumerate(pairs):
            outs.append(copy(v.at[r], o.at[r], out_sem.at[4 * i + j]))
            outs[-1].start()
    for c in outs:
        c.wait()


def row_grads(arrived, w_gate, w_up, w_down, parts=2, columns=2):
    sources, _, blocks, lanes = arrived.shape
    hidden, width = w_down.shape
    rows = sources * CAP
    struct = lambda *shape: pltpu.HBM(shape, jnp.bfloat16)
    vmem = lambda *shape: pltpu.VMEM(shape, jnp.bfloat16)
    dma = lambda n: pltpu.SemaphoreType.DMA((n,))
    return pl.pallas_call(
        functools.partial(row_grads_kernel, parts, columns),
        out_shape=(struct(rows, blocks, lanes),) + (struct(rows, hidden),) * 3,
        in_specs=[ANY, VMEM, ANY, ANY],
        out_specs=(ANY,) * 4,
        scratch_shapes=[
            vmem(width, hidden), vmem(hidden, width),
            vmem(sources, CAP, blocks, lanes), vmem(sources, CAP, blocks, lanes),
            vmem(rows, blocks, lanes), vmem(rows, hidden), vmem(rows, hidden), vmem(rows, hidden),
            dma(2), dma(parts), dma(parts), dma(4 * parts),
        ],
        compiler_params=pltpu.CompilerParams(vmem_limit_bytes=40 * 2**20),
        cost_estimate=pl.CostEstimate(
            flops=10 * rows * hidden * width, bytes_accessed=24 * 2**20, transcendentals=rows * hidden
        ),
        name="row_grads",
    )(arrived, *(
        pltpu.with_memory_space_constraint(w, space)
        for w, space in ((w_gate, pltpu.VMEM), (w_up, pltpu.HBM), (w_down, pltpu.HBM))
    ))


def combine_kernel(place, rows, out, sums):
    def one_token(t, carry):
        total = rows[place[0, t]].astype(jnp.float32)
        for k in range(1, place.shape[0]):
            total = total + rows[place[k, t]].astype(jnp.float32)
        sums[t] = total.astype(jnp.bfloat16)
        return carry

    lax.fori_loop(0, out.shape[0], one_token, 0, unroll=4)
    out[...] = sums[...].reshape(out.shape)


def combine(place, rows, tokens, width):
    return pl.pallas_call(
        combine_kernel,
        out_shape=jax.ShapeDtypeStruct((tokens, width), jnp.bfloat16),
        in_specs=[SMEM, VMEM],
        out_specs=VMEM,
        scratch_shapes=[pltpu.VMEM((tokens,) + rows.shape[1:], jnp.bfloat16)],
        compiler_params=pltpu.CompilerParams(vmem_limit_bytes=16 * 2**20),
        name="combine",
    )(place, rows)


def contract(left, right, dims):
    return lax.dot_general(left, right, (dims, ((), ())), preferred_element_type=jnp.float32)


def local(activations, out_grad, expert_ids, gate_values, w_gate, w_up, w_down):
    experts = lax.axis_size("ep")
    tokens, width = activations.shape
    lanes = (width // 128, 128)
    swap = lambda a: lax.ppermute(a, "grp", [(0, 1), (1, 0)])
    exchange = lambda a: lax.all_to_all(a, "ep", split_axis=0, concat_axis=0, tiled=True)

    send, place = fill_slots(
        expert_ids.T, gate_values.T, activations, out_grad, experts
    )
    weights = [
        jnp.concatenate([w[0], swap(w[0])], axis=axis)
        for w, axis in ((w_gate, 1), (w_up, 1), (w_down, 0))
    ]
    arrived = exchange(send).reshape((experts, 2 * CAP) + lanes)
    row_grad, weighted, grad_pre_gate, grad_pre_up = row_grads(arrived, *weights)
    returned = exchange(row_grad)

    half = w_gate.shape[2]
    x, dy = (arrived[:, i * CAP : (i + 1) * CAP].reshape(-1, width) for i in range(2))
    rows_t = ((0,), (0,))
    theirs = swap(
        (
            contract(x, grad_pre_gate[:, half:], rows_t).astype(jnp.bfloat16),
            contract(x, grad_pre_up[:, half:], rows_t).astype(jnp.bfloat16),
            contract(weighted[:, half:], dy, rows_t).astype(jnp.bfloat16),
        )
    )
    mine = (
        contract(x, grad_pre_gate[:, :half], rows_t),
        contract(x, grad_pre_up[:, :half], rows_t),
        contract(weighted[:, :half], dy, rows_t),
    )
    grads = [(m + t.astype(jnp.float32)).astype(jnp.bfloat16)[None] for m, t in zip(mine, theirs)]
    grad_input = combine(place, returned, tokens, width)
    return (grad_input, *grads)


def solution(mesh):
    tokens = P(("grp", "ep"), None)
    columns, rows = P("ep", None, "grp"), P("ep", "grp", None)
    return jax.shard_map(
        local,
        mesh=mesh,
        in_specs=(tokens, tokens, tokens, tokens, columns, columns, rows),
        out_specs=(tokens, columns, columns, rows),
        check_vma=False,
    )
```

```python
import functools

import jax
import jax.numpy as jnp
from jax import lax
from jax.experimental import pallas as pl
from jax.experimental.pallas import tpu as pltpu
from jax.sharding import PartitionSpec as P

CAP = 5
VMEM = pl.BlockSpec(memory_space=pltpu.VMEM)
ANY = pl.BlockSpec(memory_space=pl.ANY)
SMEM = pl.BlockSpec(memory_space=pltpu.SMEM)


def fill_kernel(chunks, ids, gates, x, dy, out, place, x_rows, dy_rows, v_x, v_dy, send, v_token, v_gate, token_of, gate_of, sems):
    top, tokens = ids.shape
    blocks, lanes = send.shape[1:]
    loads = [
        pltpu.make_async_copy(x, x_rows, sems.at[2 + chunks]),
        pltpu.make_async_copy(dy, dy_rows, sems.at[3 + chunks]),
    ]
    for c in loads:
        c.start()
    experts = send.shape[0] // (2 * CAP)
    f32, bf16 = jnp.float32, jnp.bfloat16
    expert_id = lax.broadcasted_iota(jnp.int32, (experts, tokens), 0)
    names = [expert_id == ids[k : k + 1, :] for k in range(top)]
    named = jnp.zeros((experts, tokens), f32)
    gate = jnp.zeros((experts, tokens), f32)
    for k in range(top):
        named = named + names[k].astype(f32)
        gate = gate + jnp.where(names[k], gates[k : k + 1, :].astype(f32), 0.0)
    before = lax.broadcasted_iota(jnp.int32, (tokens, tokens), 0) < lax.broadcasted_iota(jnp.int32, (tokens, tokens), 1)
    earlier = contract(named.astype(bf16), before.astype(f32).astype(bf16), ((1,), (0,)))
    for k in range(top):
        slot = jnp.sum(jnp.where(names[k], earlier, 0.0), axis=0, keepdims=True)
        place[k : k + 1, :] = ids[k : k + 1, :] * CAP + slot.astype(jnp.int32)
    number = lax.broadcasted_iota(jnp.int32, (8, tokens), 1).astype(f32).astype(bf16)
    ones = jnp.ones((8, tokens), bf16)
    last = ((1,), (1,))
    for c in range(CAP):
        holds = jnp.where(earlier == c, named, 0.0)
        full = contract(ones, holds.astype(bf16), last)[:1]
        token = contract(number, holds.astype(bf16), last)[:1]
        v_token[c : c + 1, :] = jnp.where(full > 0.5, token, float(tokens)).astype(jnp.int32)
        v_gate[c : c + 1, :] = contract(ones, (holds * gate).astype(bf16), last)[:1]
    tables = [
        pltpu.make_async_copy(v_token, token_of, sems.at[0]),
        pltpu.make_async_copy(v_gate, gate_of, sems.at[1]),
    ]
    for t in tables:
        t.start()
    for rows, v, load in ((x_rows, v_x, loads[0]), (dy_rows, v_dy, loads[1])):
        load.wait()
        v[pl.ds(0, tokens)] = rows[...].reshape(tokens, blocks, lanes)
        v[tokens] = jnp.zeros((blocks, lanes), bf16)
    for t in tables:
        t.wait()

    def one_expert(e, carry):
        for c in range(CAP):
            token, slot = token_of[c, e], e * (2 * CAP) + c
            send[slot] = v_x[token]
            send[slot + CAP] = (v_dy[token].astype(f32) * gate_of[c, e]).astype(bf16)
        return carry

    some = experts // chunks
    done = []
    for i in range(chunks):
        lax.fori_loop(i * some, (i + 1) * some, one_expert, 0, unroll=2)
        r = pl.ds(i * some * 2 * CAP, some * 2 * CAP)
        done.append(pltpu.make_async_copy(send.at[r], out.at[r], sems.at[2 + i]))
        done[-1].start()
    for d in done:
        d.wait()


def fill_slots(ids, gates, x, dy, experts, chunks=8):
    tokens, width = x.shape
    tile = (width // 128, 128)
    shape = (experts * 2 * CAP,) + tile
    vmem = lambda *shape: pltpu.VMEM(shape, x.dtype)
    return pl.pallas_call(
        functools.partial(fill_kernel, chunks),
        out_shape=(jax.ShapeDtypeStruct(shape, x.dtype), jax.ShapeDtypeStruct(ids.shape, jnp.int32)),
        in_specs=[VMEM, VMEM, ANY, ANY],
        out_specs=(ANY, VMEM),
        scratch_shapes=[
            vmem(tokens, width), vmem(tokens, width),
            vmem(tokens + 1, *tile), vmem(tokens + 1, *tile), vmem(*shape),
            pltpu.VMEM((8, experts), jnp.int32), pltpu.VMEM((8, experts), jnp.float32),
            pltpu.SMEM((8, experts), jnp.int32), pltpu.SMEM((8, experts), jnp.float32),
            pltpu.SemaphoreType.DMA((4 + chunks,)),
        ],
        compiler_params=pltpu.CompilerParams(vmem_limit_bytes=58 * 2**20),
        name="fill_slots",
    )(ids, gates, x, dy)


def row_grads_kernel(
    parts, columns, arrived, w_gate, up, down, out, weighted, grad_gate, grad_up,
    w_up, w_down, v_x, v_dy, v_out, v_weighted, v_grad_gate, v_grad_up, w_sem, x_sem, dy_sem, out_sem,
):
    sources, _, blocks, lanes = arrived.shape
    width = w_down.shape[1]
    some = sources // parts
    step, group = some * CAP, blocks // columns
    copy = pltpu.make_async_copy
    x_in, dy_in = [], []
    for i in range(parts):
        s = pl.ds(i * some, some)
        x_in.append(copy(arrived.at[s, pl.ds(0, CAP)], v_x.at[s], x_sem.at[i]))
        dy_in.append(copy(arrived.at[s, pl.ds(CAP, CAP)], v_dy.at[s], dy_sem.at[i]))
    up_in, down_in = copy(up, w_up, w_sem.at[0]), copy(down, w_down, w_sem.at[1])
    for c in (x_in[0], up_in, dy_in[0], down_in):
        c.start()
    for i in range(1, parts):
        x_in[i].start()
        dy_in[i].start()

    outs = []
    for i in range(parts):
        s, r = pl.ds(i * some, some), pl.ds(i * step, step)
        x_in[i].wait()
        x = v_x[s].reshape(step, width)
        pre_gate = contract(x, w_gate[...], ((1,), (0,)))
        if i == 0:
            up_in.wait()
        pre_up = contract(x, w_up[...], ((1,), (0,)))
        sig = jax.nn.sigmoid(pre_gate)
        silu = pre_gate * sig
        v_weighted[r, :] = (silu * pre_up).astype(jnp.bfloat16)
        dy_in[i].wait()
        if i == 0:
            down_in.wait()
        grad_hidden = contract(v_dy[s].reshape(step, width), w_down[...], ((1,), (1,)))
        slope = pre_up * sig * (1.0 + pre_gate * (1.0 - sig))
        v_grad_gate[r, :] = (grad_hidden * slope).astype(jnp.bfloat16)
        v_grad_up[r, :] = (grad_hidden * silu).astype(jnp.bfloat16)
        for c in range(columns):
            w = pl.ds(c * group * lanes, group * lanes)
            total = contract(v_grad_gate[r, :], w_gate[w, :], ((1,), (1,)))
            total = total + contract(v_grad_up[r, :], w_up[w, :], ((1,), (1,)))
            v_out[r, pl.ds(c * group, group), :] = total.astype(jnp.bfloat16).reshape(step, group, lanes)
        pairs = ((v_out, out), (v_weighted, weighted), (v_grad_gate, grad_gate), (v_grad_up, grad_up))
        for j, (v, o) in enumerate(pairs):
            outs.append(copy(v.at[r], o.at[r], out_sem.at[4 * i + j]))
            outs[-1].start()
    for c in outs:
        c.wait()


def row_grads(arrived, w_gate, w_up, w_down, parts=2, columns=2):
    sources, _, blocks, lanes = arrived.shape
    hidden, width = w_down.shape
    rows = sources * CAP
    struct = lambda *shape: pltpu.HBM(shape, jnp.bfloat16)
    vmem = lambda *shape: pltpu.VMEM(shape, jnp.bfloat16)
    dma = lambda n: pltpu.SemaphoreType.DMA((n,))
    return pl.pallas_call(
        functools.partial(row_grads_kernel, parts, columns),
        out_shape=(struct(rows, blocks, lanes),) + (struct(rows, hidden),) * 3,
        in_specs=[ANY, VMEM, ANY, ANY],
        out_specs=(ANY,) * 4,
        scratch_shapes=[
            vmem(width, hidden), vmem(hidden, width),
            vmem(sources, CAP, blocks, lanes), vmem(sources, CAP, blocks, lanes),
            vmem(rows, blocks, lanes), vmem(rows, hidden), vmem(rows, hidden), vmem(rows, hidden),
            dma(2), dma(parts), dma(parts), dma(4 * parts),
        ],
        compiler_params=pltpu.CompilerParams(vmem_limit_bytes=40 * 2**20),
        cost_estimate=pl.CostEstimate(
            flops=10 * rows * hidden * width, bytes_accessed=24 * 2**20, transcendentals=rows * hidden
        ),
        name="row_grads",
    )(arrived, *(
        pltpu.with_memory_space_constraint(w, space)
        for w, space in ((w_gate, pltpu.VMEM), (w_up, pltpu.HBM), (w_down, pltpu.HBM))
    ))


def combine_kernel(place, rows, out, sums):
    def one_token(t, carry):
        total = rows[place[0, t]].astype(jnp.float32)
        for k in range(1, place.shape[0]):
            total = total + rows[place[k, t]].astype(jnp.float32)
        sums[t] = total.astype(jnp.bfloat16)
        return carry

    lax.fori_loop(0, out.shape[0], one_token, 0, unroll=8)
    out[...] = sums[...].reshape(out.shape)


def combine(place, rows, tokens, width):
    return pl.pallas_call(
        combine_kernel,
        out_shape=jax.ShapeDtypeStruct((tokens, width), jnp.bfloat16),
        in_specs=[SMEM, VMEM],
        out_specs=VMEM,
        scratch_shapes=[pltpu.VMEM((tokens,) + rows.shape[1:], jnp.bfloat16)],
        compiler_params=pltpu.CompilerParams(vmem_limit_bytes=16 * 2**20),
        name="combine",
    )(place, rows)


def contract(left, right, dims):
    return lax.dot_general(left, right, (dims, ((), ())), preferred_element_type=jnp.float32)


def local(activations, out_grad, expert_ids, gate_values, w_gate, w_up, w_down):
    experts = lax.axis_size("ep")
    tokens, width = activations.shape
    lanes = (width // 128, 128)
    swap = lambda a: lax.ppermute(a, "grp", [(0, 1), (1, 0)])
    exchange = lambda a: lax.all_to_all(a, "ep", split_axis=0, concat_axis=0, tiled=True)

    send, place = fill_slots(
        expert_ids.T, gate_values.T, activations, out_grad, experts
    )
    weights = [
        jnp.concatenate([w[0], swap(w[0])], axis=axis)
        for w, axis in ((w_gate, 1), (w_up, 1), (w_down, 0))
    ]
    arrived = exchange(send).reshape((experts, 2 * CAP) + lanes)
    row_grad, weighted, grad_pre_gate, grad_pre_up = row_grads(arrived, *weights)
    returned = exchange(row_grad)

    half = w_gate.shape[2]
    x, dy = (arrived[:, i * CAP : (i + 1) * CAP].reshape(-1, width) for i in range(2))
    rows_t = ((0,), (0,))
    theirs = swap(
        (
            contract(x, grad_pre_gate[:, half:], rows_t).astype(jnp.bfloat16),
            contract(x, grad_pre_up[:, half:], rows_t).astype(jnp.bfloat16),
            contract(weighted[:, half:], dy, rows_t).astype(jnp.bfloat16),
        )
    )
    mine = (
        contract(x, grad_pre_gate[:, :half], rows_t),
        contract(x, grad_pre_up[:, :half], rows_t),
        contract(weighted[:, :half], dy, rows_t),
    )
    grads = [(m + t.astype(jnp.float32)).astype(jnp.bfloat16)[None] for m, t in zip(mine, theirs)]
    grad_input = combine(place, returned, tokens, width)
    return (grad_input, *grads)


def solution(mesh):
    tokens = P(("grp", "ep"), None)
    columns, rows = P("ep", None, "grp"), P("ep", "grp", None)
    return jax.shard_map(
        local,
        mesh=mesh,
        in_specs=(tokens, tokens, tokens, tokens, columns, columns, rows),
        out_specs=(tokens, columns, columns, rows),
        check_vma=False,
    )
```

```python
import functools

import jax
import jax.numpy as jnp
from jax import lax
from jax.experimental import pallas as pl
from jax.experimental.pallas import tpu as pltpu
from jax.sharding import PartitionSpec as P

CAP = 5
VMEM = pl.BlockSpec(memory_space=pltpu.VMEM)
ANY = pl.BlockSpec(memory_space=pl.ANY)
SMEM = pl.BlockSpec(memory_space=pltpu.SMEM)


def fill_kernel(chunks, ids, gates, x, dy, out, place, x_rows, dy_rows, v_x, v_dy, send, v_token, v_gate, token_of, gate_of, sems):
    top, tokens = ids.shape
    blocks, lanes = send.shape[1:]
    loads = [
        pltpu.make_async_copy(x, x_rows, sems.at[2 + chunks]),
        pltpu.make_async_copy(dy, dy_rows, sems.at[3 + chunks]),
    ]
    for c in loads:
        c.start()
    experts = send.shape[0] // (2 * CAP)
    f32, bf16 = jnp.float32, jnp.bfloat16
    expert_id = lax.broadcasted_iota(jnp.int32, (experts, tokens), 0)
    names = [expert_id == ids[k : k + 1, :] for k in range(top)]
    named = jnp.zeros((experts, tokens), f32)
    gate = jnp.zeros((experts, tokens), f32)
    for k in range(top):
        named = named + names[k].astype(f32)
        gate = gate + jnp.where(names[k], gates[k : k + 1, :].astype(f32), 0.0)
    before = lax.broadcasted_iota(jnp.int32, (tokens, tokens), 0) < lax.broadcasted_iota(jnp.int32, (tokens, tokens), 1)
    earlier = contract(named.astype(bf16), before.astype(f32).astype(bf16), ((1,), (0,)))
    for k in range(top):
        slot = jnp.sum(jnp.where(names[k], earlier, 0.0), axis=0, keepdims=True)
        place[k : k + 1, :] = ids[k : k + 1, :] * CAP + slot.astype(jnp.int32)
    number = lax.broadcasted_iota(jnp.int32, (8, tokens), 1).astype(f32).astype(bf16)
    ones = jnp.ones((8, tokens), bf16)
    last = ((1,), (1,))
    for c in range(CAP):
        holds = jnp.where(earlier == c, named, 0.0)
        full = contract(ones, holds.astype(bf16), last)[:1]
        token = contract(number, holds.astype(bf16), last)[:1]
        v_token[c : c + 1, :] = jnp.where(full > 0.5, token, float(tokens)).astype(jnp.int32)
        v_gate[c : c + 1, :] = contract(ones, (holds * gate).astype(bf16), last)[:1]
    tables = [
        pltpu.make_async_copy(v_token, token_of, sems.at[0]),
        pltpu.make_async_copy(v_gate, gate_of, sems.at[1]),
    ]
    for t in tables:
        t.start()
    for rows, v, load in ((x_rows, v_x, loads[0]), (dy_rows, v_dy, loads[1])):
        load.wait()
        v[pl.ds(0, tokens)] = rows[...].reshape(tokens, blocks, lanes)
        v[tokens] = jnp.zeros((blocks, lanes), bf16)
    for t in tables:
        t.wait()

    def one_expert(e, carry):
        for c in range(CAP):
            token, slot = token_of[c, e], e * (2 * CAP) + c
            send[slot] = v_x[token]
            send[slot + CAP] = (v_dy[token].astype(f32) * gate_of[c, e]).astype(bf16)
        return carry

    some = experts // chunks
    done = []
    for i in range(chunks):
        lax.fori_loop(i * some, (i + 1) * some, one_expert, 0, unroll=2)
        r = pl.ds(i * some * 2 * CAP, some * 2 * CAP)
        done.append(pltpu.make_async_copy(send.at[r], out.at[r], sems.at[2 + i]))
        done[-1].start()
    for d in done:
        d.wait()


def fill_slots(ids, gates, x, dy, experts, chunks=8):
    tokens, width = x.shape
    tile = (width // 128, 128)
    shape = (experts * 2 * CAP,) + tile
    vmem = lambda *shape: pltpu.VMEM(shape, x.dtype)
    return pl.pallas_call(
        functools.partial(fill_kernel, chunks),
        out_shape=(jax.ShapeDtypeStruct(shape, x.dtype), jax.ShapeDtypeStruct(ids.shape, jnp.int32)),
        in_specs=[VMEM, VMEM, ANY, ANY],
        out_specs=(ANY, VMEM),
        scratch_shapes=[
            vmem(tokens, width), vmem(tokens, width),
            vmem(tokens + 1, *tile), vmem(tokens + 1, *tile), vmem(*shape),
            pltpu.VMEM((8, experts), jnp.int32), pltpu.VMEM((8, experts), jnp.float32),
            pltpu.SMEM((8, experts), jnp.int32), pltpu.SMEM((8, experts), jnp.float32),
            pltpu.SemaphoreType.DMA((4 + chunks,)),
        ],
        compiler_params=pltpu.CompilerParams(vmem_limit_bytes=58 * 2**20),
        name="fill_slots",
    )(ids, gates, x, dy)


def row_grads_kernel(
    parts, columns, arrived, w_gate, up, down, out, weighted, grad_gate, grad_up,
    w_up, w_down, v_x, v_dy, v_out, v_weighted, v_grad_gate, v_grad_up, w_sem, x_sem, dy_sem, out_sem,
):
    sources, _, blocks, lanes = arrived.shape
    width = w_down.shape[1]
    some = sources // parts
    step, group = some * CAP, blocks // columns
    copy = pltpu.make_async_copy
    x_in, dy_in = [], []
    for i in range(parts):
        s = pl.ds(i * some, some)
        x_in.append(copy(arrived.at[s, pl.ds(0, CAP)], v_x.at[s], x_sem.at[i]))
        dy_in.append(copy(arrived.at[s, pl.ds(CAP, CAP)], v_dy.at[s], dy_sem.at[i]))
    up_in, down_in = copy(up, w_up, w_sem.at[0]), copy(down, w_down, w_sem.at[1])
    for c in (x_in[0], up_in, dy_in[0], down_in):
        c.start()
    for i in range(1, parts):
        x_in[i].start()
        dy_in[i].start()

    outs = []
    for i in range(parts):
        s, r = pl.ds(i * some, some), pl.ds(i * step, step)
        x_in[i].wait()
        x = v_x[s].reshape(step, width)
        pre_gate = contract(x, w_gate[...], ((1,), (0,)))
        if i == 0:
            up_in.wait()
        pre_up = contract(x, w_up[...], ((1,), (0,)))
        sig = jax.nn.sigmoid(pre_gate)
        silu = pre_gate * sig
        v_weighted[r, :] = (silu * pre_up).astype(jnp.bfloat16)
        dy_in[i].wait()
        if i == 0:
            down_in.wait()
        grad_hidden = contract(v_dy[s].reshape(step, width), w_down[...], ((1,), (1,)))
        slope = pre_up * sig * (1.0 + pre_gate * (1.0 - sig))
        v_grad_gate[r, :] = (grad_hidden * slope).astype(jnp.bfloat16)
        v_grad_up[r, :] = (grad_hidden * silu).astype(jnp.bfloat16)
        for c in range(columns):
            w = pl.ds(c * group * lanes, group * lanes)
            total = contract(v_grad_gate[r, :], w_gate[w, :], ((1,), (1,)))
            total = total + contract(v_grad_up[r, :], w_up[w, :], ((1,), (1,)))
            v_out[r, pl.ds(c * group, group), :] = total.astype(jnp.bfloat16).reshape(step, group, lanes)
        pairs = ((v_out, out), (v_weighted, weighted), (v_grad_gate, grad_gate), (v_grad_up, grad_up))
        for j, (v, o) in enumerate(pairs):
            outs.append(copy(v.at[r], o.at[r], out_sem.at[4 * i + j]))
            outs[-1].start()
    for c in outs:
        c.wait()


def row_grads(arrived, w_gate, w_up, w_down, parts=2, columns=2):
    sources, _, blocks, lanes = arrived.shape
    hidden, width = w_down.shape
    rows = sources * CAP
    struct = lambda *shape: pltpu.HBM(shape, jnp.bfloat16)
    vmem = lambda *shape: pltpu.VMEM(shape, jnp.bfloat16)
    dma = lambda n: pltpu.SemaphoreType.DMA((n,))
    return pl.pallas_call(
        functools.partial(row_grads_kernel, parts, columns),
        out_shape=(struct(rows, blocks, lanes),) + (struct(rows, hidden),) * 3,
        in_specs=[ANY, VMEM, ANY, ANY],
        out_specs=(ANY,) * 4,
        scratch_shapes=[
            vmem(width, hidden), vmem(hidden, width),
            vmem(sources, CAP, blocks, lanes), vmem(sources, CAP, blocks, lanes),
            vmem(rows, blocks, lanes), vmem(rows, hidden), vmem(rows, hidden), vmem(rows, hidden),
            dma(2), dma(parts), dma(parts), dma(4 * parts),
        ],
        compiler_params=pltpu.CompilerParams(vmem_limit_bytes=40 * 2**20),
        cost_estimate=pl.CostEstimate(
            flops=10 * rows * hidden * width, bytes_accessed=24 * 2**20, transcendentals=rows * hidden
        ),
        name="row_grads",
    )(arrived, *(
        pltpu.with_memory_space_constraint(w, space)
        for w, space in ((w_gate, pltpu.VMEM), (w_up, pltpu.HBM), (w_down, pltpu.HBM))
    ))


def combine_kernel(chunks, place, rows, out, sums, v_out, sems):
    def one_token(t, carry):
        total = rows[place[0, t]].astype(jnp.float32)
        for k in range(1, place.shape[0]):
            total = total + rows[place[k, t]].astype(jnp.float32)
        sums[t] = total.astype(jnp.bfloat16)
        return carry

    some, width = out.shape[0] // chunks, out.shape[1]
    done = []
    for i in range(chunks):
        lax.fori_loop(i * some, (i + 1) * some, one_token, 0, unroll=8)
        r = pl.ds(i * some, some)
        v_out[r, :] = sums[r].reshape(some, width)
        done.append(pltpu.make_async_copy(v_out.at[r], out.at[r], sems.at[i]))
        done[-1].start()
    for d in done:
        d.wait()


def combine(place, rows, tokens, width, chunks=4):
    return pl.pallas_call(
        functools.partial(combine_kernel, chunks),
        out_shape=jax.ShapeDtypeStruct((tokens, width), jnp.bfloat16),
        in_specs=[SMEM, VMEM],
        out_specs=ANY,
        scratch_shapes=[
            pltpu.VMEM((tokens,) + rows.shape[1:], jnp.bfloat16),
            pltpu.VMEM((tokens, width), jnp.bfloat16),
            pltpu.SemaphoreType.DMA((chunks,)),
        ],
        compiler_params=pltpu.CompilerParams(vmem_limit_bytes=16 * 2**20),
        name="combine",
    )(place, rows)


def contract(left, right, dims):
    return lax.dot_general(left, right, (dims, ((), ())), preferred_element_type=jnp.float32)


def local(activations, out_grad, expert_ids, gate_values, w_gate, w_up, w_down):
    experts = lax.axis_size("ep")
    tokens, width = activations.shape
    lanes = (width // 128, 128)
    swap = lambda a: lax.ppermute(a, "grp", [(0, 1), (1, 0)])
    exchange = lambda a: lax.all_to_all(a, "ep", split_axis=0, concat_axis=0, tiled=True)

    send, place = fill_slots(
        expert_ids.T, gate_values.T, activations, out_grad, experts
    )
    weights = [
        jnp.concatenate([w[0], swap(w[0])], axis=axis)
        for w, axis in ((w_gate, 1), (w_up, 1), (w_down, 0))
    ]
    arrived = exchange(send).reshape((experts, 2 * CAP) + lanes)
    row_grad, weighted, grad_pre_gate, grad_pre_up = row_grads(arrived, *weights)
    returned = exchange(row_grad)

    half = w_gate.shape[2]
    x, dy = (arrived[:, i * CAP : (i + 1) * CAP].reshape(-1, width) for i in range(2))
    rows_t = ((0,), (0,))
    theirs = swap(
        (
            contract(x, grad_pre_gate[:, half:], rows_t).astype(jnp.bfloat16),
            contract(x, grad_pre_up[:, half:], rows_t).astype(jnp.bfloat16),
            contract(weighted[:, half:], dy, rows_t).astype(jnp.bfloat16),
        )
    )
    mine = (
        contract(x, grad_pre_gate[:, :half], rows_t),
        contract(x, grad_pre_up[:, :half], rows_t),
        contract(weighted[:, :half], dy, rows_t),
    )
    grads = [(m + t.astype(jnp.float32)).astype(jnp.bfloat16)[None] for m, t in zip(mine, theirs)]
    grad_input = combine(place, returned, tokens, width)
    return (grad_input, *grads)


def solution(mesh):
    tokens = P(("grp", "ep"), None)
    columns, rows = P("ep", None, "grp"), P("ep", "grp", None)
    return jax.shard_map(
        local,
        mesh=mesh,
        in_specs=(tokens, tokens, tokens, tokens, columns, columns, rows),
        out_specs=(tokens, columns, columns, rows),
        check_vma=False,
    )
```
